32 devices in a mesh: tm: 8 (over y, x, core), head: 4 (over z).
Axes of the slice: x: 2, y: 2, z: 4, core: 2. Of those that a mesh axis runs over, the one named last changes fastest.
Arguments:
- queries: bfloat16 [1024, 2048], P(('tm', 'head')), may hold values from -120 to 120
- keys: bfloat16 [1024, 2048], P(('tm', 'head')), may hold values from -5 to 5
- values: bfloat16 [1024, 2048], P(('tm', 'head'))
- history: bfloat16 [8, 4, 32, 512], P('tm'), may hold values from -6 to 6
- fine_proj: bfloat16 [512, 4096], P(None, 'head'), may hold values from -0.25 to 0.25
- coarse_proj: bfloat16 [4096, 4096], P(None, 'head'), may hold values from -0.09375 to 0.09375
- frame_counts: int32 [8], replicated, may hold values from 1 to 4, as said below
- levels: int32 [8], replicated, may hold values from 0 to 1, as said below
Outputs:
- attended: bfloat16 [1024, 2048], P(('tm', 'head'))
The draws below stay inside these ranges and needn't reach their ends.
Inputs may be any that keep to these rules, and one draw needn't show every extreme that they name: `frame_counts`: some group with level 0 holds all 4 frames. `levels`: both kernels occur.
All inputs are finite; a program needn't handle non-finite values.
Results may differ from the reference program's by a relative error of at most 0.0073.
Values may be sent and summed in bfloat16 or wider, within the bound.
A program may use at most 128 MiB of HBM per device.

```python
import math
import jax
import jax.numpy as jnp
from jax import lax

HD = 128
HEADS = 16
C = 16
GF = 4
HL = 32
WL = 32
PAIRS = 4096
TOKENS = 1024
GROUPS = 8
P0 = 512
P1 = 4096


def shared_keys(key):
    base = jnp.clip(jax.random.normal(key, (TOKENS, HEADS * HD), jnp.float32), -4.0, 4.0)
    noise = jnp.clip(jax.random.normal(jax.random.fold_in(key, 91), (TOKENS, HEADS * HD), jnp.float32), -4.0, 4.0)
    period = min(509, TOKENS)
    leading = (jnp.arange(TOKENS) % period == 1)[:, None]
    return jnp.where(leading, jnp.roll(base, 1, axis=0) + 0.15 * noise, base)


def group_plan(key):
    first = jax.random.randint(jax.random.fold_in(key, 11), (), 0, GROUPS)
    second = (first + 1 + jax.random.randint(jax.random.fold_in(key, 12), (), 0, GROUPS - 1)) % GROUPS
    counts = jax.random.randint(jax.random.fold_in(key, 13), (GROUPS,), 1, GF + 1)
    kinds = jax.random.randint(jax.random.fold_in(key, 14), (GROUPS,), 0, 2)
    places = jnp.arange(GROUPS)
    counts = jnp.where(places == first, GF, counts)
    kinds = jnp.where(places == first, 0, jnp.where(places == second, 1, kinds))
    return (counts.astype(jnp.int32), kinds.astype(jnp.int32))


def draw_keys(key, part):
    shaped = shared_keys(key)
    return shaped.astype(jnp.bfloat16)


def draw_queries(key, part):
    key = jax.random.fold_in(key, 5)
    own = 3.0 * jnp.clip(jax.random.normal(key, (TOKENS, HEADS * HD), jnp.float32), -4.0, 4.0)
    return own.astype(jnp.bfloat16)


def draw_values(key, part):
    key = jax.random.fold_in(key, 9)
    drawn = jnp.clip(jax.random.normal(key, (TOKENS, HEADS * HD), jnp.float32), -6.0, 6.0)
    return drawn.astype(jnp.bfloat16)


def draw_frame_counts(key, part):
    plan = group_plan(key)
    return plan[0]


def draw_levels(key, part):
    plan = group_plan(key)
    return plan[1]


def shard_levels(key, extent, pieces, least, high):
    loudness, own = 1.0, jax.random.fold_in(key, 6)
    for position, parts in pieces:
        draws = jnp.exp(jax.random.uniform(jax.random.fold_in(own, position), (parts,), jnp.float32, least / len(pieces), high / len(pieces)))
        loudness = loudness * jnp.repeat(draws, extent[position] // parts).reshape([-1 if axis == position else 1 for axis in range(len(extent))])
    return loudness


def scatter_about(stream_key, shape, spread, bound, cuts=(), kind=jnp.bfloat16):
    result = jax.random.normal(stream_key, shape, jnp.float32) * spread
    if len(cuts) > 0:
        result = shard_levels(stream_key, shape, cuts, -0.22, 0.18) * result
    return jnp.clip(result, min=-bound, max=bound).astype(kind)


def setup_inputs(seed: int = 0) -> dict:
    splits = jax.random.split(jax.random.key(seed), 9)
    return {
        "queries": draw_queries(jax.random.fold_in(splits[8], 71), 0),
        "keys": draw_keys(jax.random.fold_in(splits[8], 71), 0),
        "values": draw_values(jax.random.fold_in(splits[8], 71), 0),
        "history": scatter_about(splits[3], (GROUPS, GF, HL, WL * C), 1.0, 6.0, ((0, 8),)),
        "fine_proj": scatter_about(splits[4], (P0, PAIRS), P0 ** -0.5, 0.25, ((1, 4),)),
        "coarse_proj": scatter_about(splits[5], (P1, PAIRS), P1 ** -0.5, 0.09375, ((1, 4),)),
        "frame_counts": draw_frame_counts(jax.random.fold_in(splits[8], 71), 0),
        "levels": draw_levels(jax.random.fold_in(splits[8], 71), 0),
    }


very_low = -1e+30

def patch_tokens(history, counts, levels, fine_proj, coarse_proj):
    groups, frames, rows, merged = history.shape
    channels = fine_proj.shape[0] // 32
    columns = merged // channels
    live = jnp.arange(frames, dtype=jnp.int32)[None, :] < counts[:, None]
    masked = jnp.where(live[:, :, None, None], history, jnp.zeros((), history.dtype))
    fine = masked.reshape(groups, frames // 2, 2, rows // 4, 4, columns // 4, 4, channels)
    fine = fine.transpose(0, 1, 3, 5, 2, 4, 6, 7).reshape(-1, 32 * channels)
    coarse = masked.reshape(groups, 4, rows // 8, 8, columns // 8, 8, channels)
    coarse = coarse.transpose(0, 2, 4, 1, 3, 5, 6).reshape(-1, 256 * channels)
    fine_pairs = jnp.dot(fine, fine_proj, preferred_element_type=jnp.float32).astype(jnp.bfloat16)
    coarse_pairs = jnp.dot(coarse, coarse_proj, preferred_element_type=jnp.float32).astype(jnp.bfloat16)
    slots = frames // 2 * (rows // 4) * (columns // 4)
    coarse_count = rows // 8 * (columns // 8)
    width = fine_proj.shape[1]
    fine_pairs = fine_pairs.reshape(groups, slots, width)
    coarse_pairs = coarse_pairs.reshape(groups, coarse_count, width)
    padding = jnp.zeros((groups, slots - coarse_count, width), jnp.bfloat16)
    coarse_full = jnp.concatenate([coarse_pairs, padding], axis=1)
    return jnp.where((levels == 0)[:, None, None], fine_pairs, coarse_full)

def slot_valid(counts, levels, slots):
    index = jnp.arange(slots, dtype=jnp.int32)[None, :]
    fine_live = 2 * (index // (slots // 2)) < counts[:, None]
    coarse_live = index < slots // 8
    return jnp.where(levels[:, None] == 0, fine_live, coarse_live)

def reference(queries, keys, values, history, fine_proj, coarse_proj, frame_counts, levels):
    tokens = queries.shape[0]
    hist_pairs = patch_tokens(history, frame_counts, levels, fine_proj, coarse_proj)
    hist_live = slot_valid(frame_counts, levels, hist_pairs.shape[1]).reshape(-1)
    split = hist_pairs.reshape(-1, HEADS, 2, HD)
    all_keys = jnp.concatenate([keys.reshape(tokens, HEADS, HD), split[:, :, 0]], axis=0).transpose(1, 0, 2)
    all_values = jnp.concatenate([values.reshape(tokens, HEADS, HD), split[:, :, 1]], axis=0).transpose(1, 0, 2)
    usable = jnp.concatenate([jnp.ones((tokens,), jnp.bool_), hist_live])
    head_queries = queries.reshape(tokens, HEADS, HD).transpose(1, 0, 2)
    block = math.gcd(tokens, 1024)

    def one_head(operands):
        head_q, head_k, head_v = operands

        def one_block(query_block):
            scores = jnp.dot(query_block, head_k.T, preferred_element_type=jnp.float32) * (1.0 / math.sqrt(HD))
            masked = jnp.where(usable[None, :], scores, very_low)
            highest = lax.optimization_barrier(jnp.max(masked, axis=1, keepdims=True))
            expo = jnp.where(usable[None, :], jnp.exp(masked - highest), 0.0)
            denom = lax.optimization_barrier(jnp.sum(expo, axis=1, keepdims=True))
            weights = expo.astype(jnp.bfloat16)
            mixed = jnp.dot(weights, head_v, preferred_element_type=jnp.float32) / denom
            return mixed.astype(jnp.bfloat16)
        return lax.map(one_block, head_q.reshape(-1, block, HD)).reshape(tokens, HD)
    output = lax.map(one_head, (head_queries, all_keys, all_values))
    return output.transpose(1, 0, 2).reshape(tokens, HEADS * HD)
```

```python
import functools
import math

import jax
import jax.numpy as jnp
from jax import lax
from jax.experimental import pallas as pl
from jax.experimental.pallas import tpu as pltpu
from jax.sharding import PartitionSpec as P

HD = 128
HEADS = 16
FRAMES = 4
ROWS = 32
LANES = 512
SLOTS = 128
COARSE = 16
KCHUNKS = 4
QBLOCK = 256

very_low = -1e30
LOG2E = 1.4426950408889634
MESH = pl.DeviceIdType.MESH


def loop(count, step):
    if count <= 4:
        for index in range(count):
            step(index)
    else:

        def one(index, carry):
            step(index)
            return carry

        lax.fori_loop(0, count, one, 0)


def kernel(
    nz,
    tm,
    q_ref,
    k_ref,
    v_ref,
    h_ref,
    fw_ref,
    cw_ref,
    cnt_ref,
    lev_ref,
    out_ref,
    qbuf,
    kvbuf,
    hist,
    hp,
    hv,
    h32,
    p32,
    w2,
    cw,
    res,
    obuf,
    m_ref,
    l_ref,
    acc_ref,
    send_sem,
    recv_sem,
    own_sem,
    fsend,
    frecv,
    hsend,
    hrecv,
    gsend,
    grecv,
    osend,
    orecv,
    wsem,
    fsem,
    hsem,
):
    local = q_ref.shape[0]
    per_plane = HEADS // nz
    sibs = tm // per_plane
    t = lax.axis_index("tm")
    z = lax.axis_index("head")
    j = lax.div(t, sibs)
    s = lax.rem(t, sibs)
    me = z * per_plane + j
    kdepth = cw.shape[0] // KCHUNKS

    hist_load = pltpu.make_async_copy(h_ref.at[0], hv, hsem)
    hist_load.start()
    fine_loads = []
    for i in range(8):
        for half in range(2):
            fine_loads.append(
                pltpu.make_async_copy(
                    fw_ref.at[pl.ds(i * 64, 64)],
                    w2.at[pl.ds(i * 128 + half * 64, 64)],
                    fsem.at[i, half],
                )
            )
    coarse_loads = [
        pltpu.make_async_copy(
            cw_ref.at[pl.ds(i * kdepth, kdepth)], cw.at[pl.ds(i * kdepth, kdepth)], wsem.at[i]
        )
        for i in range(KCHUNKS)
    ]

    def device(head, sib):
        plane = lax.div(head, per_plane)
        return (lax.rem(head, per_plane) * sibs + sib, plane)

    z_order = sorted(range(nz), key=lambda d: -min(d, nz - d))
    peers = []
    for dz in z_order:
        for dj in range(per_plane):
            if dz or dj:
                pz = lax.rem(z + dz, nz)
                peers.append((dz, pz * per_plane + lax.rem(j + dj, per_plane)))

    def sib_of(d):
        return lax.rem(s + 1 + d, sibs)

    barrier = pltpu.get_barrier_semaphore()
    for _, p in peers:
        pl.semaphore_signal(barrier, inc=1, device_id=device(p, s), device_id_type=MESH)

    def greet(d):
        pl.semaphore_signal(barrier, inc=1, device_id=device(me, sib_of(d)), device_id_type=MESH)

    loop(sibs - 1, greet)
    for load in fine_loads:
        load.start()
    for load in coarse_loads:
        load.start()
    pl.semaphore_wait(barrier, HEADS - 1 + sibs - 1)

    def columns(head):
        return pl.ds(pl.multiple_of(head * HD, HD), HD)

    def rows_of(head):
        return pl.ds(pl.multiple_of(head * local, local), local)

    def targets(row):
        return (
            qbuf.at[rows_of(row)],
            kvbuf.at[s, rows_of(row), pl.ds(0, HD)],
            kvbuf.at[s, rows_of(row), pl.ds(HD, HD)],
        )

    def qkv(p):
        return [
            pltpu.make_async_remote_copy(
                src_ref=src.at[:, columns(p)],
                dst_ref=dst,
                send_sem=send_sem.at[p, n],
                recv_sem=recv_sem.at[me, n],
                device_id=device(p, s),
                device_id_type=MESH,
            )
            for n, (src, dst) in enumerate(zip((q_ref, k_ref, v_ref), targets(me)))
        ]

    def qkv_in(p):
        return [
            pltpu.make_async_remote_copy(
                src_ref=src.at[:, columns(p)],
                dst_ref=dst,
                send_sem=send_sem.at[p, n],
                recv_sem=recv_sem.at[p, n],
                device_id=device(p, s),
                device_id_type=MESH,
            )
            for n, (src, dst) in enumerate(zip((q_ref, k_ref, v_ref), targets(p)))
        ]

    for _, p in peers:
        for copy in qkv(p):
            copy.start()
    own = [
        pltpu.make_async_copy(src.at[:, columns(me)], dst, own_sem.at[n])
        for n, (src, dst) in enumerate(zip((q_ref, k_ref, v_ref), targets(me)))
    ]
    for copy in own:
        copy.start()

    count = cnt_ref[t]
    level = lev_ref[t]
    hist_load.wait()
    blocks = LANES // HD
    for f in range(FRAMES):
        for cb in range(blocks):
            piece = hv[f, :, cb * HD : (cb + 1) * HD].astype(jnp.float32)
            h32[f, cb] = jnp.where(f < count, piece, 0.0)
    for f in range(FRAMES):
        for r in range(8):
            for cb in range(blocks):
                p32[cb * 4 : cb * 4 + 4, (f * 8 + r) * HD : (f * 8 + r + 1) * HD] = h32[
                    f, cb, pl.ds(r, 4, stride=8)
                ]
    lane_low = lax.broadcasted_iota(jnp.int32, (32, HD), 1) < HD // 2
    parts = []
    for ff in range(2):
        for r in range(4):
            stack = []
            for big in range(2):
                x = jnp.concatenate(
                    [
                        h32[big * 2 + ff, cb, pl.ds(r, 8, stride=4)]
                        for cb in range(blocks)
                    ],
                    axis=0,
                )
                stack.append(jnp.where(lane_low, x, 0.0))
                stack.append(jnp.where(lane_low, 0.0, x))
            parts.append(jnp.concatenate(stack, axis=0).astype(jnp.bfloat16))
    fine_in = jnp.concatenate(parts, axis=1)
    for load in fine_loads:
        load.wait()
    for jj in range(per_plane):
        h_cols = slice(jj * 2 * HD, (jj + 1) * 2 * HD)
        fine = jnp.dot(fine_in, w2[:, h_cols], preferred_element_type=jnp.float32)
        hp[jj] = fine.astype(jnp.bfloat16)
    total = None
    for i in range(KCHUNKS):
        coarse_loads[i].wait()
        part = jnp.dot(
            p32[:, i * kdepth : (i + 1) * kdepth].astype(jnp.bfloat16),
            cw[i * kdepth : (i + 1) * kdepth, :],
            preferred_element_type=jnp.float32,
        )
        total = part if total is None else total + part
    for jj in range(per_plane):
        coarse = total[:, jj * 2 * HD : (jj + 1) * 2 * HD].astype(jnp.bfloat16)
        full = jnp.concatenate(
            [coarse, jnp.zeros((SLOTS - COARSE, 2 * HD), jnp.bfloat16)], axis=0
        )
        hp[jj] = jnp.where(level == 0, hp[jj], full)

    def slot_rows(index):
        return pl.ds(pl.multiple_of(index * SLOTS, SLOTS), SLOTS)

    def hist_copy(pj, slot):
        return pltpu.make_async_remote_copy(
            src_ref=hp.at[pj],
            dst_ref=hist.at[s, slot_rows(slot)],
            send_sem=hsend.at[pj],
            recv_sem=hrecv.at[slot],
            device_id=(pj * sibs + s, z),
            device_id_type=MESH,
        )

    for dj in range(1, per_plane):
        hist_copy(lax.rem(j + dj, per_plane), j).start()
    hist[s, slot_rows(j)] = hp[j]

    def plane_rows(pz):
        size = per_plane * local
        return pl.ds(pl.multiple_of(pz * size, size), size)

    def forward(pz, part, d):
        return pltpu.make_async_remote_copy(
            src_ref=kvbuf.at[part, plane_rows(pz)],
            dst_ref=kvbuf.at[part, plane_rows(pz)],
            send_sem=fsend.at[pz, d],
            recv_sem=frecv.at[part, pz],
            device_id=device(me, sib_of(d)),
            device_id_type=MESH,
        )

    def forward_hist(part, d):
        return pltpu.make_async_remote_copy(
            src_ref=hist.at[part],
            dst_ref=hist.at[part],
            send_sem=gsend.at[d],
            recv_sem=grecv.at[part],
            device_id=device(me, sib_of(d)),
            device_id_type=MESH,
        )

    for copy in own:
        copy.wait()
    for dz in [0] + z_order[:-1]:
        pz = lax.rem(z + dz, nz)
        for other, p in peers:
            if other == dz:
                for copy in qkv_in(p):
                    copy.wait_recv()
        loop(sibs - 1, lambda d: forward(pz, s, d).start())
    for dj in range(1, per_plane):
        pj = lax.rem(j + dj, per_plane)
        hist_copy(pj, pj).wait_recv()
    loop(sibs - 1, lambda d: forward_hist(s, d).start())

    factor = LOG2E / math.sqrt(HD)
    queries = HEADS * local

    def absorb(qb, pair, bias, first):
        rows = pl.ds(qb * QBLOCK, QBLOCK)
        scores = lax.dot_general(
            qbuf[rows],
            pair[:, :HD],
            (((1,), (1,)), ((), ())),
            preferred_element_type=jnp.float32,
        )
        if bias is not None:
            scores = scores + bias
        top = jnp.max(scores, axis=1, keepdims=True)
        if not first:
            old = m_ref[rows]
            top = jnp.maximum(old[:, :1], top)
        expo = jnp.exp2((scores - top) * factor)
        total = jnp.sum(expo, axis=1, keepdims=True)
        update = jnp.dot(
            expo.astype(jnp.bfloat16), pair[:, HD:], preferred_element_type=jnp.float32
        )
        wide = jnp.broadcast_to(top, (QBLOCK, HD))
        if first:
            l_ref[rows] = jnp.broadcast_to(total, (QBLOCK, HD))
            acc_ref[rows] = update
        else:
            shrink = jnp.exp2((old - wide) * factor)
            l_ref[rows] = l_ref[rows] * shrink + total
            acc_ref[rows] = acc_ref[rows] * shrink + update
        m_ref[rows] = wide

    def token_chunk(part, first):
        for qb in range(queries // QBLOCK):
            absorb(qb, kvbuf[part], None, first)

    def hist_bias(part):
        index = lax.broadcasted_iota(jnp.int32, (1, SLOTS), 1)
        pieces = []
        for jj in range(per_plane):
            g = jj * sibs + part
            fine_rows = jnp.where(cnt_ref[g] > 2, SLOTS, SLOTS // 2)
            live = jnp.where(lev_ref[g] == 0, fine_rows, COARSE)
            pieces.append(jnp.where(index < live, 0.0, very_low))
        return jnp.concatenate(pieces, axis=1)

    def hist_chunk(part):
        bias = hist_bias(part)
        for qb in range(queries // QBLOCK):
            absorb(qb, hist[part], bias, False)

    token_chunk(s, True)
    hist_chunk(s)

    def rest(d):
        part = sib_of(d)
        for pz in range(nz):
            forward(pz, part, d).wait_recv()
        token_chunk(part, False)
        forward_hist(part, d).wait_recv()
        hist_chunk(part)

    loop(sibs - 1, rest)

    def out_copy(p, slot):
        return pltpu.make_async_remote_copy(
            src_ref=res.at[rows_of(p)],
            dst_ref=obuf.at[slot],
            send_sem=osend.at[p],
            recv_sem=orecv.at[slot],
            device_id=device(p, s),
            device_id_type=MESH,
        )

    res[...] = (acc_ref[...] / l_ref[...]).astype(jnp.bfloat16)
    for _, p in peers:
        out_copy(p, me).start()
    obuf[me] = res[rows_of(me)]
    for _, p in peers:
        out_copy(p, p).wait_recv()
    for h in range(HEADS):
        out_ref[:, h * HD : (h + 1) * HD] = obuf[h]

    for _, p in peers:
        for copy in qkv(p):
            copy.wait_send()
        out_copy(p, me).wait_send()
    for dj in range(1, per_plane):
        hist_copy(lax.rem(j + dj, per_plane), j).wait_send()
    for pz in range(nz):
        loop(sibs - 1, lambda d: forward(pz, s, d).wait_send())
    loop(sibs - 1, lambda d: forward_hist(s, d).wait_send())


def body(nz, tm, queries, keys, values, history, fine_proj, coarse_proj, frame_counts, levels):
    local, width = queries.shape
    per_plane = HEADS // nz
    sibs = tm // per_plane
    heads_width = fine_proj.shape[1]
    bf16, f32 = jnp.bfloat16, jnp.float32
    rows = HEADS * local
    dma = pltpu.SemaphoreType.DMA
    others = max(sibs - 1, 1)
    return pl.pallas_call(
        functools.partial(kernel, nz, tm),
        out_shape=jax.ShapeDtypeStruct((local, width), bf16),
        in_specs=[pl.BlockSpec(memory_space=pl.ANY)] * 6
        + [pl.BlockSpec(memory_space=pltpu.SMEM)] * 2,
        out_specs=pl.BlockSpec(memory_space=pltpu.VMEM),
        scratch_shapes=[
            pltpu.VMEM((rows, HD), bf16),
            pltpu.VMEM((sibs, rows, 2 * HD), bf16),
            pltpu.VMEM((sibs, per_plane * SLOTS, 2 * HD), bf16),
            pltpu.VMEM((per_plane, SLOTS, 2 * HD), bf16),
            pltpu.VMEM((FRAMES, ROWS, LANES), bf16),
            pltpu.VMEM((FRAMES, LANES // HD, ROWS, HD), f32),
            pltpu.VMEM((COARSE, coarse_proj.shape[0]), f32),
            pltpu.VMEM((2 * fine_proj.shape[0], heads_width), bf16),
            pltpu.VMEM(coarse_proj.shape, bf16),
            pltpu.VMEM((rows, HD), bf16),
            pltpu.VMEM((HEADS, local, HD), bf16),
            pltpu.VMEM((rows, HD), f32),
            pltpu.VMEM((rows, HD), f32),
            pltpu.VMEM((rows, HD), f32),
            dma((HEADS, 3)),
            dma((HEADS, 3)),
            dma((3,)),
            dma((nz, others)),
            dma((sibs, nz)),
            dma((per_plane,)),
            dma((per_plane,)),
            dma((others,)),
            dma((sibs,)),
            dma((HEADS,)),
            dma((HEADS,)),
            dma((KCHUNKS,)),
            dma((8, 2)),
            dma(()),
        ],
        compiler_params=pltpu.CompilerParams(
            collective_id=0, has_side_effects=True, vmem_limit_bytes=56 * 1024 * 1024
        ),
        cost_estimate=pl.CostEstimate(
            flops=700_000_000, bytes_accessed=12_000_000, transcendentals=1_100_000
        ),
    )(queries, keys, values, history, fine_proj, coarse_proj, frame_counts, levels)


def solution(mesh):
    in_specs = (
        P(("tm", "head"), None),
        P(("tm", "head"), None),
        P(("tm", "head"), None),
        P("tm", None, None, None),
        P(None, "head"),
        P(None, "head"),
        P(),
        P(),
    )
    out_specs = P(("tm", "head"), None)
    nz, tm = mesh.shape["head"], mesh.shape["tm"]
    return jax.shard_map(
        functools.partial(body, nz, tm),
        mesh=mesh,
        in_specs=in_specs,
        out_specs=out_specs,
        check_vma=False,
    )
```

```python
import functools
import math

import jax
import jax.numpy as jnp
from jax import lax
from jax.experimental import pallas as pl
from jax.experimental.pallas import tpu as pltpu
from jax.sharding import PartitionSpec as P

HD = 128
HEADS = 16
FRAMES = 4
ROWS = 32
LANES = 512
SLOTS = 128
COARSE = 16
KCHUNKS = 4
QBLOCK = 256

very_low = -1e30
LOG2E = 1.4426950408889634
MESH = pl.DeviceIdType.MESH


def loop(count, step):
    if count <= 4:
        for index in range(count):
            step(index)
    else:

        def one(index, carry):
            step(index)
            return carry

        lax.fori_loop(0, count, one, 0)


def kernel(
    nz,
    tm,
    q_ref,
    k_ref,
    v_ref,
    h_ref,
    fw_ref,
    cw_ref,
    cnt_ref,
    lev_ref,
    out_ref,
    inbuf,
    pack,
    recv,
    hist,
    hp,
    hv,
    h32,
    p32,
    w2,
    cw,
    res,
    obuf,
    m_ref,
    l_ref,
    acc_ref,
    send_sem,
    recv_sem,
    in_sem,
    fsend,
    frecv,
    hsend,
    hrecv,
    gsend,
    grecv,
    osend,
    orecv,
    wsem,
    fsem,
    hsem,
):
    local = q_ref.shape[0]
    per_plane = HEADS // nz
    sibs = tm // per_plane
    t = lax.axis_index("tm")
    z = lax.axis_index("head")
    j = lax.div(t, sibs)
    s = lax.rem(t, sibs)
    me = z * per_plane + j
    kdepth = cw.shape[0] // KCHUNKS

    in_loads = [
        pltpu.make_async_copy(src, inbuf.at[n], in_sem.at[n])
        for n, src in enumerate((q_ref, k_ref, v_ref))
    ]
    hist_load = pltpu.make_async_copy(h_ref.at[0], hv, hsem)
    for load in in_loads:
        load.start()
    hist_load.start()
    fine_loads = []
    for i in range(8):
        for half in range(2):
            fine_loads.append(
                pltpu.make_async_copy(
                    fw_ref.at[pl.ds(i * 64, 64)],
                    w2.at[pl.ds(i * 128 + half * 64, 64)],
                    fsem.at[i, half],
                )
            )
    coarse_loads = [
        pltpu.make_async_copy(
            cw_ref.at[pl.ds(i * kdepth, kdepth)], cw.at[pl.ds(i * kdepth, kdepth)], wsem.at[i]
        )
        for i in range(KCHUNKS)
    ]

    def device(head, sib):
        plane = lax.div(head, per_plane)
        return (lax.rem(head, per_plane) * sibs + sib, plane)

    z_order = sorted(range(nz), key=lambda d: -min(d, nz - d))
    peers = []
    for dz in z_order:
        for dj in range(per_plane):
            if dz or dj:
                pz = lax.rem(z + dz, nz)
                peers.append((dz, pz * per_plane + lax.rem(j + dj, per_plane)))

    def sib_of(d):
        return lax.rem(s + 1 + d, sibs)

    barrier = pltpu.get_barrier_semaphore()
    for _, p in peers:
        pl.semaphore_signal(barrier, inc=1, device_id=device(p, s), device_id_type=MESH)

    def greet(d):
        pl.semaphore_signal(barrier, inc=1, device_id=device(me, sib_of(d)), device_id_type=MESH)

    loop(sibs - 1, greet)
    for load in fine_loads:
        load.start()
    for load in coarse_loads:
        load.start()
    for n, load in enumerate(in_loads):
        load.wait()
        for h in range(HEADS):
            pack[h, n * local : (n + 1) * local, :] = inbuf[n, :, h * HD : (h + 1) * HD]
    pl.semaphore_wait(barrier, HEADS - 1 + sibs - 1)

    def rows_of(head):
        return pl.ds(pl.multiple_of(head * local, local), local)

    def qkv(p, slot):
        return pltpu.make_async_remote_copy(
            src_ref=pack.at[p],
            dst_ref=recv.at[s, slot],
            send_sem=send_sem.at[p],
            recv_sem=recv_sem.at[slot],
            device_id=device(p, s),
            device_id_type=MESH,
        )

    for _, p in peers:
        qkv(p, me).start()
    recv[s, me] = pack[me]

    count = cnt_ref[t]
    level = lev_ref[t]
    hist_load.wait()
    blocks = LANES // HD
    for f in range(FRAMES):
        for cb in range(blocks):
            piece = hv[f, :, cb * HD : (cb + 1) * HD].astype(jnp.float32)
            h32[f, cb] = jnp.where(f < count, piece, 0.0)
    for f in range(FRAMES):
        for r in range(8):
            for cb in range(blocks):
                p32[cb * 4 : cb * 4 + 4, (f * 8 + r) * HD : (f * 8 + r + 1) * HD] = h32[
                    f, cb, pl.ds(r, 4, stride=8)
                ]
    lane_low = lax.broadcasted_iota(jnp.int32, (32, HD), 1) < HD // 2
    parts = []
    for ff in range(2):
        for r in range(4):
            stack = []
            for big in range(2):
                x = jnp.concatenate(
                    [
                        h32[big * 2 + ff, cb, pl.ds(r, 8, stride=4)]
                        for cb in range(blocks)
                    ],
                    axis=0,
                )
                stack.append(jnp.where(lane_low, x, 0.0))
                stack.append(jnp.where(lane_low, 0.0, x))
            parts.append(jnp.concatenate(stack, axis=0).astype(jnp.bfloat16))
    fine_in = jnp.concatenate(parts, axis=1)
    for load in fine_loads:
        load.wait()
    for jj in range(per_plane):
        h_cols = slice(jj * 2 * HD, (jj + 1) * 2 * HD)
        fine = jnp.dot(fine_in, w2[:, h_cols], preferred_element_type=jnp.float32)
        hp[jj] = fine.astype(jnp.bfloat16)
    total = None
    for i in range(KCHUNKS):
        coarse_loads[i].wait()
        part = jnp.dot(
            p32[:, i * kdepth : (i + 1) * kdepth].astype(jnp.bfloat16),
            cw[i * kdepth : (i + 1) * kdepth, :],
            preferred_element_type=jnp.float32,
        )
        total = part if total is None else total + part
    for jj in range(per_plane):
        coarse = total[:, jj * 2 * HD : (jj + 1) * 2 * HD].astype(jnp.bfloat16)
        full = jnp.concatenate(
            [coarse, jnp.zeros((SLOTS - COARSE, 2 * HD), jnp.bfloat16)], axis=0
        )
        hp[jj] = jnp.where(level == 0, hp[jj], full)

    def slot_rows(index):
        return pl.ds(pl.multiple_of(index * SLOTS, SLOTS), SLOTS)

    def hist_copy(pj, slot):
        return pltpu.make_async_remote_copy(
            src_ref=hp.at[pj],
            dst_ref=hist.at[s, slot_rows(slot)],
            send_sem=hsend.at[pj],
            recv_sem=hrecv.at[slot],
            device_id=(pj * sibs + s, z),
            device_id_type=MESH,
        )

    for dj in range(1, per_plane):
        hist_copy(lax.rem(j + dj, per_plane), j).start()
    hist[s, slot_rows(j)] = hp[j]

    def forward(pz, part, d):
        block = recv.at[
            part, pl.ds(pz * per_plane, per_plane), pl.ds(local, 2 * local)
        ]
        return pltpu.make_async_remote_copy(
            src_ref=block,
            dst_ref=block,
            send_sem=fsend.at[pz, d],
            recv_sem=frecv.at[part, pz],
            device_id=device(me, sib_of(d)),
            device_id_type=MESH,
        )

    def forward_hist(part, d):
        return pltpu.make_async_remote_copy(
            src_ref=hist.at[part],
            dst_ref=hist.at[part],
            send_sem=gsend.at[d],
            recv_sem=grecv.at[part],
            device_id=device(me, sib_of(d)),
            device_id_type=MESH,
        )

    for dz in [0] + z_order[:-1]:
        pz = lax.rem(z + dz, nz)
        for other, p in peers:
            if other == dz:
                qkv(p, p).wait_recv()
        loop(sibs - 1, lambda d: forward(pz, s, d).start())
    for dj in range(1, per_plane):
        pj = lax.rem(j + dj, per_plane)
        hist_copy(pj, pj).wait_recv()
    loop(sibs - 1, lambda d: forward_hist(s, d).start())

    factor = LOG2E / math.sqrt(HD)
    queries = HEADS * local

    def queries_in(qb):
        heads = QBLOCK // local
        block = recv[s, qb * heads : (qb + 1) * heads, 0:local, :]
        return block.reshape(QBLOCK, HD)

    def absorb(qb, keys, values, bias, first):
        rows = pl.ds(qb * QBLOCK, QBLOCK)
        scores = lax.dot_general(
            queries_in(qb),
            keys,
            (((1,), (1,)), ((), ())),
            preferred_element_type=jnp.float32,
        )
        if bias is not None:
            scores = scores + bias
        top = jnp.max(scores, axis=1, keepdims=True)
        if not first:
            old = m_ref[rows]
            top = jnp.maximum(old[:, :1], top)
        expo = jnp.exp2((scores - top) * factor)
        total = jnp.sum(expo, axis=1, keepdims=True)
        update = jnp.dot(
            expo.astype(jnp.bfloat16), values, preferred_element_type=jnp.float32
        )
        wide = jnp.broadcast_to(top, (QBLOCK, HD))
        if first:
            l_ref[rows] = jnp.broadcast_to(total, (QBLOCK, HD))
            acc_ref[rows] = update
        else:
            shrink = jnp.exp2((old - wide) * factor)
            l_ref[rows] = l_ref[rows] * shrink + total
            acc_ref[rows] = acc_ref[rows] * shrink + update
        m_ref[rows] = wide

    def token_chunk(part, first):
        keys = recv[part, :, local : 2 * local, :].reshape(queries, HD)
        values = recv[part, :, 2 * local : 3 * local, :].reshape(queries, HD)
        for qb in range(queries // QBLOCK):
            absorb(qb, keys, values, None, first)

    def hist_bias(part):
        index = lax.broadcasted_iota(jnp.int32, (1, SLOTS), 1)
        pieces = []
        for jj in range(per_plane):
            g = jj * sibs + part
            fine_rows = jnp.where(cnt_ref[g] > 2, SLOTS, SLOTS // 2)
            live = jnp.where(lev_ref[g] == 0, fine_rows, COARSE)
            pieces.append(jnp.where(index < live, 0.0, very_low))
        return jnp.concatenate(pieces, axis=1)

    def hist_chunk(part):
        bias = hist_bias(part)
        for qb in range(queries // QBLOCK):
            absorb(qb, hist[part, :, :HD], hist[part, :, HD:], bias, False)

    token_chunk(s, True)
    hist_chunk(s)

    def rest(d):
        part = sib_of(d)
        for pz in range(nz):
            forward(pz, part, d).wait_recv()
        token_chunk(part, False)
        forward_hist(part, d).wait_recv()
        hist_chunk(part)

    loop(sibs - 1, rest)

    def out_copy(p, slot):
        return pltpu.make_async_remote_copy(
            src_ref=res.at[rows_of(p)],
            dst_ref=obuf.at[slot],
            send_sem=osend.at[p],
            recv_sem=orecv.at[slot],
            device_id=device(p, s),
            device_id_type=MESH,
        )

    res[...] = (acc_ref[...] / l_ref[...]).astype(jnp.bfloat16)
    for _, p in peers:
        out_copy(p, me).start()
    obuf[me] = res[rows_of(me)]
    for _, p in peers:
        out_copy(p, p).wait_recv()
    for h in range(HEADS):
        out_ref[:, h * HD : (h + 1) * HD] = obuf[h]

    for _, p in peers:
        qkv(p, me).wait_send()
        out_copy(p, me).wait_send()
    for dj in range(1, per_plane):
        hist_copy(lax.rem(j + dj, per_plane), j).wait_send()
    for pz in range(nz):
        loop(sibs - 1, lambda d: forward(pz, s, d).wait_send())
    loop(sibs - 1, lambda d: forward_hist(s, d).wait_send())


def body(nz, tm, queries, keys, values, history, fine_proj, coarse_proj, frame_counts, levels):
    local, width = queries.shape
    per_plane = HEADS // nz
    sibs = tm // per_plane
    heads_width = fine_proj.shape[1]
    bf16, f32 = jnp.bfloat16, jnp.float32
    rows = HEADS * local
    dma = pltpu.SemaphoreType.DMA
    others = max(sibs - 1, 1)
    return pl.pallas_call(
        functools.partial(kernel, nz, tm),
        out_shape=pltpu.VMEM((local, width), bf16),
        in_specs=[pl.BlockSpec(memory_space=pl.ANY)] * 6
        + [pl.BlockSpec(memory_space=pltpu.SMEM)] * 2,
        out_specs=pl.BlockSpec(memory_space=pltpu.VMEM),
        scratch_shapes=[
            pltpu.VMEM((3, local, width), bf16),
            pltpu.VMEM((HEADS, 3 * local, HD), bf16),
            pltpu.VMEM((sibs, HEADS, 3 * local, HD), bf16),
            pltpu.VMEM((sibs, per_plane * SLOTS, 2 * HD), bf16),
            pltpu.VMEM((per_plane, SLOTS, 2 * HD), bf16),
            pltpu.VMEM((FRAMES, ROWS, LANES), bf16),
            pltpu.VMEM((FRAMES, LANES // HD, ROWS, HD), f32),
            pltpu.VMEM((COARSE, coarse_proj.shape[0]), f32),
            pltpu.VMEM((2 * fine_proj.shape[0], heads_width), bf16),
            pltpu.VMEM(coarse_proj.shape, bf16),
            pltpu.VMEM((rows, HD), bf16),
            pltpu.VMEM((HEADS, local, HD), bf16),
            pltpu.VMEM((rows, HD), f32),
            pltpu.VMEM((rows, HD), f32),
            pltpu.VMEM((rows, HD), f32),
            dma((HEADS,)),
            dma((HEADS,)),
            dma((3,)),
            dma((nz, others)),
            dma((sibs, nz)),
            dma((per_plane,)),
            dma((per_plane,)),
            dma((others,)),
            dma((sibs,)),
            dma((HEADS,)),
            dma((HEADS,)),
            dma((KCHUNKS,)),
            dma((8, 2)),
            dma(()),
        ],
        compiler_params=pltpu.CompilerParams(
            collective_id=0, has_side_effects=True, vmem_limit_bytes=56 * 1024 * 1024
        ),
        cost_estimate=pl.CostEstimate(
            flops=700_000_000, bytes_accessed=12_000_000, transcendentals=1_100_000
        ),
    )(queries, keys, values, history, fine_proj, coarse_proj, frame_counts, levels)


def solution(mesh):
    in_specs = (
        P(("tm", "head"), None),
        P(("tm", "head"), None),
        P(("tm", "head"), None),
        P("tm", None, None, None),
        P(None, "head"),
        P(None, "head"),
        P(),
        P(),
    )
    out_specs = P(("tm", "head"), None)
    nz, tm = mesh.shape["head"], mesh.shape["tm"]
    return jax.shard_map(
        functools.partial(body, nz, tm),
        mesh=mesh,
        in_specs=in_specs,
        out_specs=out_specs,
        check_vma=False,
    )
```

```python
import functools
import math

import jax
import jax.numpy as jnp
from jax import lax
from jax.experimental import pallas as pl
from jax.experimental.pallas import tpu as pltpu
from jax.sharding import PartitionSpec as P

HD = 128
HEADS = 16
FRAMES = 4
ROWS = 32
LANES = 512
SLOTS = 128
COARSE = 16
KCHUNKS = 4

very_low = -1e30
LOG2E = 1.4426950408889634
MESH = pl.DeviceIdType.MESH


def loop(count, step):
    if count <= 4:
        for index in range(count):
            step(index)
    else:

        def one(index, carry):
            step(index)
            return carry

        lax.fori_loop(0, count, one, 0)


def kernel(
    nz,
    tm,
    q_ref,
    k_ref,
    v_ref,
    h_ref,
    fw_ref,
    cw_ref,
    cnt_ref,
    lev_ref,
    out_ref,
    inbuf,
    pack,
    recv,
    hist,
    hp,
    hv,
    h32,
    p32,
    w2,
    cw,
    res,
    obuf,
    m_ref,
    l_ref,
    acc_ref,
    send_sem,
    recv_sem,
    in_sem,
    fsend,
    frecv,
    hsend,
    hrecv,
    gsend,
    grecv,
    osend,
    orecv,
    wsem,
    fsem,
    hsem,
):
    local = q_ref.shape[0]
    per_plane = HEADS // nz
    sibs = tm // per_plane
    t = lax.axis_index("tm")
    z = lax.axis_index("head")
    j = lax.div(t, sibs)
    s = lax.rem(t, sibs)
    me = z * per_plane + j
    kdepth = cw.shape[0] // KCHUNKS

    in_loads = [
        pltpu.make_async_copy(src, inbuf.at[n], in_sem.at[n])
        for n, src in enumerate((q_ref, k_ref, v_ref))
    ]
    hist_load = pltpu.make_async_copy(h_ref.at[0], hv, hsem)
    for load in in_loads:
        load.start()
    hist_load.start()
    fine_loads = []
    for i in range(8):
        for half in range(2):
            fine_loads.append(
                pltpu.make_async_copy(
                    fw_ref.at[pl.ds(i * 64, 64)],
                    w2.at[pl.ds(i * 128 + half * 64, 64)],
                    fsem.at[i, half],
                )
            )
    coarse_loads = [
        pltpu.make_async_copy(
            cw_ref.at[pl.ds(i * kdepth, kdepth)], cw.at[pl.ds(i * kdepth, kdepth)], wsem.at[i]
        )
        for i in range(KCHUNKS)
    ]

    def device(head, sib):
        plane = lax.div(head, per_plane)
        return (lax.rem(head, per_plane) * sibs + sib, plane)

    half = HEADS // 2
    near = lax.div(me, half)
    far = 1 - near
    far_peers = [far * half + lax.rem(me + i, half) for i in range(half)]
    near_peers = [near * half + lax.rem(me + i, half) for i in range(1, half)]
    peers = far_peers + near_peers

    def sib_of(d):
        return lax.rem(s + 1 + d, sibs)

    barrier = pltpu.get_barrier_semaphore()
    for p in peers:
        pl.semaphore_signal(barrier, inc=1, device_id=device(p, s), device_id_type=MESH)

    def greet(d):
        pl.semaphore_signal(barrier, inc=1, device_id=device(me, sib_of(d)), device_id_type=MESH)

    loop(sibs - 1, greet)
    for load in fine_loads:
        load.start()
    for load in coarse_loads:
        load.start()
    for n, load in enumerate(in_loads):
        load.wait()
        for h in range(HEADS):
            pack[h, n * local : (n + 1) * local, :] = inbuf[n, :, h * HD : (h + 1) * HD]
    pl.semaphore_wait(barrier, HEADS - 1 + sibs - 1)

    def rows_of(head):
        return pl.ds(pl.multiple_of(head * local, local), local)

    def qkv(p, slot):
        return pltpu.make_async_remote_copy(
            src_ref=pack.at[p],
            dst_ref=recv.at[s, slot],
            send_sem=send_sem.at[p],
            recv_sem=recv_sem.at[slot],
            device_id=device(p, s),
            device_id_type=MESH,
        )

    for p in peers:
        qkv(p, me).start()
    recv[s, me] = pack[me]

    count = cnt_ref[t]
    level = lev_ref[t]
    hist_load.wait()
    blocks = LANES // HD
    for f in range(FRAMES):
        for cb in range(blocks):
            piece = hv[f, :, cb * HD : (cb + 1) * HD].astype(jnp.float32)
            h32[f, cb] = jnp.where(f < count, piece, 0.0)
    for f in range(FRAMES):
        for r in range(8):
            for cb in range(blocks):
                p32[cb * 4 : cb * 4 + 4, (f * 8 + r) * HD : (f * 8 + r + 1) * HD] = h32[
                    f, cb, pl.ds(r, 4, stride=8)
                ]
    lane_low = lax.broadcasted_iota(jnp.int32, (32, HD), 1) < HD // 2
    parts = []
    for ff in range(2):
        for r in range(4):
            stack = []
            for big in range(2):
                x = jnp.concatenate(
                    [
                        h32[big * 2 + ff, cb, pl.ds(r, 8, stride=4)]
                        for cb in range(blocks)
                    ],
                    axis=0,
                )
                stack.append(jnp.where(lane_low, x, 0.0))
                stack.append(jnp.where(lane_low, 0.0, x))
            parts.append(jnp.concatenate(stack, axis=0).astype(jnp.bfloat16))
    fine_in = jnp.concatenate(parts, axis=1)
    for load in fine_loads:
        load.wait()
    for jj in range(per_plane):
        h_cols = slice(jj * 2 * HD, (jj + 1) * 2 * HD)
        fine = jnp.dot(fine_in, w2[:, h_cols], preferred_element_type=jnp.float32)
        hp[jj] = fine.astype(jnp.bfloat16)
    total = None
    for i in range(KCHUNKS):
        coarse_loads[i].wait()
        part = jnp.dot(
            p32[:, i * kdepth : (i + 1) * kdepth].astype(jnp.bfloat16),
            cw[i * kdepth : (i + 1) * kdepth, :],
            preferred_element_type=jnp.float32,
        )
        total = part if total is None else total + part
    for jj in range(per_plane):
        coarse = total[:, jj * 2 * HD : (jj + 1) * 2 * HD].astype(jnp.bfloat16)
        full = jnp.concatenate(
            [coarse, jnp.zeros((SLOTS - COARSE, 2 * HD), jnp.bfloat16)], axis=0
        )
        hp[jj] = jnp.where(level == 0, hp[jj], full)

    def slot_rows(index):
        return pl.ds(pl.multiple_of(index * SLOTS, SLOTS), SLOTS)

    def hist_copy(pj, slot):
        return pltpu.make_async_remote_copy(
            src_ref=hp.at[pj],
            dst_ref=hist.at[s, slot_rows(slot)],
            send_sem=hsend.at[pj],
            recv_sem=hrecv.at[slot],
            device_id=(pj * sibs + s, z),
            device_id_type=MESH,
        )

    for dj in range(1, per_plane):
        hist_copy(lax.rem(j + dj, per_plane), j).start()
    hist[s, slot_rows(j)] = hp[j]

    def forward(side, part, d):
        block = recv.at[
            part, pl.ds(side * half, half), pl.ds(local, 2 * local)
        ]
        return pltpu.make_async_remote_copy(
            src_ref=block,
            dst_ref=block,
            send_sem=fsend.at[side, d],
            recv_sem=frecv.at[part, side],
            device_id=device(me, sib_of(d)),
            device_id_type=MESH,
        )

    def forward_hist(part, d):
        return pltpu.make_async_remote_copy(
            src_ref=hist.at[part],
            dst_ref=hist.at[part],
            send_sem=gsend.at[d],
            recv_sem=grecv.at[part],
            device_id=device(me, sib_of(d)),
            device_id_type=MESH,
        )

    factor = LOG2E / math.sqrt(HD)
    queries = HEADS * local
    block_rows = half * local

    def queries_in(qb):
        block = recv[s, pl.ds(qb * half, half), 0:local, :]
        return block.reshape(block_rows, HD)

    def absorb(qb, keys, values, bias, first):
        rows = pl.ds(pl.multiple_of(qb * block_rows, block_rows), block_rows)
        scores = lax.dot_general(
            queries_in(qb),
            keys,
            (((1,), (1,)), ((), ())),
            preferred_element_type=jnp.float32,
        )
        if bias is not None:
            scores = scores + bias
        top = jnp.max(scores, axis=1, keepdims=True)
        if not first:
            old = m_ref[rows]
            top = jnp.maximum(old[:, :1], top)
        expo = jnp.exp2((scores - top) * factor)
        total = jnp.sum(expo, axis=1, keepdims=True)
        update = jnp.dot(
            expo.astype(jnp.bfloat16), values, preferred_element_type=jnp.float32
        )
        wide = jnp.broadcast_to(top, (block_rows, HD))
        if first:
            l_ref[rows] = jnp.broadcast_to(total, (block_rows, HD))
            acc_ref[rows] = update
        else:
            shrink = jnp.exp2((old - wide) * factor)
            l_ref[rows] = l_ref[rows] * shrink + total
            acc_ref[rows] = acc_ref[rows] * shrink + update
        m_ref[rows] = wide

    def token_chunk(qb, part):
        keys = recv[part, :, local : 2 * local, :].reshape(queries, HD)
        values = recv[part, :, 2 * local : 3 * local, :].reshape(queries, HD)
        absorb(qb, keys, values, None, False)

    def hist_bias(part):
        index = lax.broadcasted_iota(jnp.int32, (1, SLOTS), 1)
        pieces = []
        for jj in range(per_plane):
            g = jj * sibs + part
            fine_rows = jnp.where(cnt_ref[g] > 2, SLOTS, SLOTS // 2)
            live = jnp.where(lev_ref[g] == 0, fine_rows, COARSE)
            pieces.append(jnp.where(index < live, 0.0, very_low))
        return jnp.concatenate(pieces, axis=1)

    def hist_chunk(qb, part, first):
        bias = hist_bias(part)
        absorb(qb, hist[part, :, :HD], hist[part, :, HD:], bias, first)

    def out_copy(p, slot):
        return pltpu.make_async_remote_copy(
            src_ref=res.at[rows_of(p)],
            dst_ref=obuf.at[slot],
            send_sem=osend.at[p],
            recv_sem=orecv.at[slot],
            device_id=device(p, s),
            device_id_type=MESH,
        )

    def finish(qb, heads):
        rows = pl.ds(pl.multiple_of(qb * block_rows, block_rows), block_rows)
        res[rows] = (acc_ref[rows] / l_ref[rows]).astype(jnp.bfloat16)
        for p in heads:
            out_copy(p, me).start()

    for p in near_peers:
        qkv(p, p).wait_recv()
    loop(sibs - 1, lambda d: forward(near, s, d).start())
    for dj in range(1, per_plane):
        pj = lax.rem(j + dj, per_plane)
        hist_copy(pj, pj).wait_recv()
    loop(sibs - 1, lambda d: forward_hist(s, d).start())
    hist_chunk(near, s, True)
    for p in far_peers:
        qkv(p, p).wait_recv()
    loop(sibs - 1, lambda d: forward(far, s, d).start())

    hist_chunk(far, s, True)
    token_chunk(far, s)

    def far_rest(d):
        part = sib_of(d)
        forward_hist(part, d).wait_recv()
        hist_chunk(far, part, False)
        for side in range(2):
            forward(side, part, d).wait_recv()
        token_chunk(far, part)

    loop(sibs - 1, far_rest)
    finish(far, far_peers)
    token_chunk(near, s)

    def near_rest(d):
        part = sib_of(d)
        hist_chunk(near, part, False)
        token_chunk(near, part)

    loop(sibs - 1, near_rest)
    finish(near, near_peers)
    obuf[me] = res[rows_of(me)]
    for p in peers:
        out_copy(p, p).wait_recv()
    for h in range(HEADS):
        out_ref[:, h * HD : (h + 1) * HD] = obuf[h]

    for p in peers:
        qkv(p, me).wait_send()
        out_copy(p, me).wait_send()
    for dj in range(1, per_plane):
        hist_copy(lax.rem(j + dj, per_plane), j).wait_send()
    for side in range(2):
        loop(sibs - 1, lambda d: forward(side, s, d).wait_send())
    loop(sibs - 1, lambda d: forward_hist(s, d).wait_send())


def body(nz, tm, queries, keys, values, history, fine_proj, coarse_proj, frame_counts, levels):
    local, width = queries.shape
    per_plane = HEADS // nz
    sibs = tm // per_plane
    heads_width = fine_proj.shape[1]
    bf16, f32 = jnp.bfloat16, jnp.float32
    rows = HEADS * local
    dma = pltpu.SemaphoreType.DMA
    others = max(sibs - 1, 1)
    return pl.pallas_call(
        functools.partial(kernel, nz, tm),
        out_shape=pltpu.VMEM((local, width), bf16),
        in_specs=[pl.BlockSpec(memory_space=pl.ANY)] * 6
        + [pl.BlockSpec(memory_space=pltpu.SMEM)] * 2,
        out_specs=pl.BlockSpec(memory_space=pltpu.VMEM),
        scratch_shapes=[
            pltpu.VMEM((3, local, width), bf16),
            pltpu.VMEM((HEADS, 3 * local, HD), bf16),
            pltpu.VMEM((sibs, HEADS, 3 * local, HD), bf16),
            pltpu.VMEM((sibs, per_plane * SLOTS, 2 * HD), bf16),
            pltpu.VMEM((per_plane, SLOTS, 2 * HD), bf16),
            pltpu.VMEM((FRAMES, ROWS, LANES), bf16),
            pltpu.VMEM((FRAMES, LANES // HD, ROWS, HD), f32),
            pltpu.VMEM((COARSE, coarse_proj.shape[0]), f32),
            pltpu.VMEM((2 * fine_proj.shape[0], heads_width), bf16),
            pltpu.VMEM(coarse_proj.shape, bf16),
            pltpu.VMEM((rows, HD), bf16),
            pltpu.VMEM((HEADS, local, HD), bf16),
            pltpu.VMEM((rows, HD), f32),
            pltpu.VMEM((rows, HD), f32),
            pltpu.VMEM((rows, HD), f32),
            dma((HEADS,)),
            dma((HEADS,)),
            dma((3,)),
            dma((2, others)),
            dma((sibs, 2)),
            dma((per_plane,)),
            dma((per_plane,)),
            dma((others,)),
            dma((sibs,)),
            dma((HEADS,)),
            dma((HEADS,)),
            dma((KCHUNKS,)),
            dma((8, 2)),
            dma(()),
        ],
        compiler_params=pltpu.CompilerParams(
            collective_id=0, has_side_effects=True, vmem_limit_bytes=56 * 1024 * 1024
        ),
        cost_estimate=pl.CostEstimate(
            flops=700_000_000, bytes_accessed=12_000_000, transcendentals=1_100_000
        ),
    )(queries, keys, values, history, fine_proj, coarse_proj, frame_counts, levels)


def solution(mesh):
    in_specs = (
        P(("tm", "head"), None),
        P(("tm", "head"), None),
        P(("tm", "head"), None),
        P("tm", None, None, None),
        P(None, "head"),
        P(None, "head"),
        P(),
        P(),
    )
    out_specs = P(("tm", "head"), None)
    nz, tm = mesh.shape["head"], mesh.shape["tm"]
    return jax.shard_map(
        functools.partial(body, nz, tm),
        mesh=mesh,
        in_specs=in_specs,
        out_specs=out_specs,
        check_vma=False,
    )
```

```python
import functools
import math

import jax
import jax.numpy as jnp
from jax import lax
from jax.experimental import pallas as pl
from jax.experimental.pallas import tpu as pltpu
from jax.sharding import PartitionSpec as P

HD = 128
HEADS = 16
FRAMES = 4
ROWS = 32
LANES = 512
SLOTS = 128
COARSE = 16
KCHUNKS = 4

very_low = -1e30
LOG2E = 1.4426950408889634
MESH = pl.DeviceIdType.MESH


def loop(count, step):
    if count <= 4:
        for index in range(count):
            step(index)
    else:

        def one(index, carry):
            step(index)
            return carry

        lax.fori_loop(0, count, one, 0)


def kernel(
    nz,
    tm,
    q_ref,
    k_ref,
    v_ref,
    h_ref,
    fw_ref,
    cw_ref,
    cnt_ref,
    lev_ref,
    out_ref,
    inbuf,
    pack,
    recv,
    hist,
    hp,
    hv,
    h32,
    p32,
    w2,
    cw,
    res,
    obuf,
    m_ref,
    l_ref,
    acc_ref,
    send_sem,
    recv_sem,
    in_sem,
    fsend,
    frecv,
    hsend,
    hrecv,
    gsend,
    grecv,
    osend,
    orecv,
    wsem,
    fsem,
    hsem,
):
    local = q_ref.shape[0]
    per_plane = HEADS // nz
    sibs = tm // per_plane
    t = lax.axis_index("tm")
    z = lax.axis_index("head")
    j = lax.div(t, sibs)
    s = lax.rem(t, sibs)
    me = z * per_plane + j
    kdepth = cw.shape[0] // KCHUNKS

    in_loads = [
        pltpu.make_async_copy(src, inbuf.at[n], in_sem.at[n])
        for n, src in enumerate((q_ref, k_ref, v_ref))
    ]
    hist_load = pltpu.make_async_copy(h_ref.at[0], hv, hsem)
    for load in in_loads:
        load.start()
    hist_load.start()
    fine_loads = []
    for i in range(8):
        for half in range(2):
            fine_loads.append(
                pltpu.make_async_copy(
                    fw_ref.at[pl.ds(i * 64, 64)],
                    w2.at[pl.ds(i * 128 + half * 64, 64)],
                    fsem.at[i, half],
                )
            )
    coarse_loads = [
        pltpu.make_async_copy(
            cw_ref.at[pl.ds(i * kdepth, kdepth)], cw.at[pl.ds(i * kdepth, kdepth)], wsem.at[i]
        )
        for i in range(KCHUNKS)
    ]

    def device(head, sib):
        plane = lax.div(head, per_plane)
        return (lax.rem(head, per_plane) * sibs + sib, plane)

    half = HEADS // 2
    near = lax.div(me, half)
    far = 1 - near
    far_peers = [far * half + lax.rem(me + i, half) for i in range(half)]
    near_peers = [near * half + lax.rem(me + i, half) for i in range(1, half)]
    peers = far_peers + near_peers

    def sib_of(d):
        return lax.rem(s + 1 + d, sibs)

    barrier = pltpu.get_barrier_semaphore()
    for p in peers:
        pl.semaphore_signal(barrier, inc=1, device_id=device(p, s), device_id_type=MESH)

    def greet(d):
        pl.semaphore_signal(barrier, inc=1, device_id=device(me, sib_of(d)), device_id_type=MESH)

    loop(sibs - 1, greet)
    for load in fine_loads:
        load.start()
    for load in coarse_loads:
        load.start()
    for n, load in enumerate(in_loads):
        load.wait()
        for h in range(HEADS):
            pack[h, n * local : (n + 1) * local, :] = inbuf[n, :, h * HD : (h + 1) * HD]
    pl.semaphore_wait(barrier, HEADS - 1 + sibs - 1)

    def rows_of(head):
        return pl.ds(pl.multiple_of(head * local, local), local)

    def qkv(p, slot):
        return pltpu.make_async_remote_copy(
            src_ref=pack.at[p],
            dst_ref=recv.at[s, slot],
            send_sem=send_sem.at[p],
            recv_sem=recv_sem.at[slot],
            device_id=device(p, s),
            device_id_type=MESH,
        )

    for p in peers:
        qkv(p, me).start()
    recv[s, me] = pack[me]

    count = cnt_ref[t]
    level = lev_ref[t]
    hist_load.wait()
    blocks = LANES // HD
    for f in range(FRAMES):
        for cb in range(blocks):
            piece = hv[f, :, cb * HD : (cb + 1) * HD].astype(jnp.float32)
            h32[f, cb] = jnp.where(f < count, piece, 0.0)
    for f in range(FRAMES):
        for r in range(8):
            for cb in range(blocks):
                p32[cb * 4 : cb * 4 + 4, (f * 8 + r) * HD : (f * 8 + r + 1) * HD] = h32[
                    f, cb, pl.ds(r, 4, stride=8)
                ]
    lane_low = lax.broadcasted_iota(jnp.int32, (32, HD), 1) < HD // 2
    parts = []
    for ff in range(2):
        for r in range(4):
            stack = []
            for big in range(2):
                x = jnp.concatenate(
                    [
                        h32[big * 2 + ff, cb, pl.ds(r, 8, stride=4)]
                        for cb in range(blocks)
                    ],
                    axis=0,
                )
                stack.append(jnp.where(lane_low, x, 0.0))
                stack.append(jnp.where(lane_low, 0.0, x))
            parts.append(jnp.concatenate(stack, axis=0).astype(jnp.bfloat16))
    fine_in = jnp.concatenate(parts, axis=1)
    for load in fine_loads:
        load.wait()
    for jj in range(per_plane):
        h_cols = slice(jj * 2 * HD, (jj + 1) * 2 * HD)
        fine = jnp.dot(fine_in, w2[:, h_cols], preferred_element_type=jnp.float32)
        hp[jj] = fine.astype(jnp.bfloat16)
    total = None
    for i in range(KCHUNKS):
        coarse_loads[i].wait()
        part = jnp.dot(
            p32[:, i * kdepth : (i + 1) * kdepth].astype(jnp.bfloat16),
            cw[i * kdepth : (i + 1) * kdepth, :],
            preferred_element_type=jnp.float32,
        )
        total = part if total is None else total + part
    for jj in range(per_plane):
        coarse = total[:, jj * 2 * HD : (jj + 1) * 2 * HD].astype(jnp.bfloat16)
        full = jnp.concatenate(
            [coarse, jnp.zeros((SLOTS - COARSE, 2 * HD), jnp.bfloat16)], axis=0
        )
        hp[jj] = jnp.where(level == 0, hp[jj], full)

    def slot_rows(index):
        return pl.ds(pl.multiple_of(index * SLOTS, SLOTS), SLOTS)

    def hist_copy(pj, slot):
        return pltpu.make_async_remote_copy(
            src_ref=hp.at[pj],
            dst_ref=hist.at[s, slot_rows(slot)],
            send_sem=hsend.at[pj],
            recv_sem=hrecv.at[slot],
            device_id=(pj * sibs + s, z),
            device_id_type=MESH,
        )

    for dj in range(1, per_plane):
        hist_copy(lax.rem(j + dj, per_plane), j).start()
    hist[s, slot_rows(j)] = hp[j]

    def forward(side, part, d):
        block = recv.at[
            part, pl.ds(side * half, half), pl.ds(local, 2 * local)
        ]
        return pltpu.make_async_remote_copy(
            src_ref=block,
            dst_ref=block,
            send_sem=fsend.at[side, d],
            recv_sem=frecv.at[part, side],
            device_id=device(me, sib_of(d)),
            device_id_type=MESH,
        )

    def forward_hist(part, d):
        return pltpu.make_async_remote_copy(
            src_ref=hist.at[part],
            dst_ref=hist.at[part],
            send_sem=gsend.at[d],
            recv_sem=grecv.at[part],
            device_id=device(me, sib_of(d)),
            device_id_type=MESH,
        )

    factor = LOG2E / math.sqrt(HD)
    queries = HEADS * local
    block_rows = half * local

    def queries_in(qb):
        block = recv[s, pl.ds(qb * half, half), 0:local, :]
        return block.reshape(block_rows, HD)

    def absorb(qb, keys, values, bias, first):
        rows = pl.ds(pl.multiple_of(qb * block_rows, block_rows), block_rows)
        scores = lax.dot_general(
            queries_in(qb),
            keys,
            (((1,), (1,)), ((), ())),
            preferred_element_type=jnp.float32,
        )
        if bias is not None:
            scores = scores + bias
        top = jnp.max(scores, axis=1, keepdims=True)
        if not first:
            old = m_ref[rows]
            top = jnp.maximum(old[:, :1], top)
        expo = jnp.exp2((scores - top) * factor)
        total = jnp.sum(expo, axis=1, keepdims=True)
        update = jnp.dot(
            expo.astype(jnp.bfloat16), values, preferred_element_type=jnp.float32
        )
        wide = jnp.broadcast_to(top, (block_rows, HD))
        if first:
            l_ref[rows] = jnp.broadcast_to(total, (block_rows, HD))
            acc_ref[rows] = update
        else:
            shrink = jnp.exp2((old - wide) * factor)
            l_ref[rows] = l_ref[rows] * shrink + total
            acc_ref[rows] = acc_ref[rows] * shrink + update
        m_ref[rows] = wide

    def token_chunk(qb, part):
        keys = recv[part, :, local : 2 * local, :].reshape(queries, HD)
        values = recv[part, :, 2 * local : 3 * local, :].reshape(queries, HD)
        absorb(qb, keys, values, None, False)

    def hist_bias(part):
        index = lax.broadcasted_iota(jnp.int32, (1, SLOTS), 1)
        pieces = []
        for jj in range(per_plane):
            g = jj * sibs + part
            fine_rows = jnp.where(cnt_ref[g] > 2, SLOTS, SLOTS // 2)
            live = jnp.where(lev_ref[g] == 0, fine_rows, COARSE)
            pieces.append(jnp.where(index < live, 0.0, very_low))
        return jnp.concatenate(pieces, axis=1)

    def hist_chunk(qb, part, first):
        bias = hist_bias(part)
        absorb(qb, hist[part, :, :HD], hist[part, :, HD:], bias, first)

    def out_copy(p, slot):
        return pltpu.make_async_remote_copy(
            src_ref=res.at[rows_of(p)],
            dst_ref=obuf.at[slot],
            send_sem=osend.at[p],
            recv_sem=orecv.at[slot],
            device_id=device(p, s),
            device_id_type=MESH,
        )

    def finish(qb, heads):
        rows = pl.ds(pl.multiple_of(qb * block_rows, block_rows), block_rows)
        res[rows] = (acc_ref[rows] / l_ref[rows]).astype(jnp.bfloat16)
        for p in heads:
            out_copy(p, me).start()

    for p in near_peers:
        qkv(p, p).wait_recv()
    loop(sibs - 1, lambda d: forward(near, s, d).start())
    for dj in range(1, per_plane):
        pj = lax.rem(j + dj, per_plane)
        hist_copy(pj, pj).wait_recv()
    loop(sibs - 1, lambda d: forward_hist(s, d).start())
    hist_chunk(near, s, True)

    def near_history(d):
        part = sib_of(d)
        forward_hist(part, d).wait_recv()
        hist_chunk(near, part, False)

    loop(sibs - 1, near_history)
    for p in far_peers:
        qkv(p, p).wait_recv()
    loop(sibs - 1, lambda d: forward(far, s, d).start())

    hist_chunk(far, s, True)
    token_chunk(far, s)

    def far_rest(d):
        part = sib_of(d)
        hist_chunk(far, part, False)
        for side in range(2):
            forward(side, part, d).wait_recv()
        token_chunk(far, part)

    loop(sibs - 1, far_rest)
    finish(far, far_peers)
    token_chunk(near, s)

    def near_rest(d):
        token_chunk(near, sib_of(d))

    loop(sibs - 1, near_rest)
    finish(near, near_peers)
    obuf[me] = res[rows_of(me)]
    for p in peers:
        out_copy(p, p).wait_recv()
    for h in range(HEADS):
        out_ref[:, h * HD : (h + 1) * HD] = obuf[h]

    for p in peers:
        qkv(p, me).wait_send()
        out_copy(p, me).wait_send()
    for dj in range(1, per_plane):
        hist_copy(lax.rem(j + dj, per_plane), j).wait_send()
    for side in range(2):
        loop(sibs - 1, lambda d: forward(side, s, d).wait_send())
    loop(sibs - 1, lambda d: forward_hist(s, d).wait_send())


def body(nz, tm, queries, keys, values, history, fine_proj, coarse_proj, frame_counts, levels):
    local, width = queries.shape
    per_plane = HEADS // nz
    sibs = tm // per_plane
    heads_width = fine_proj.shape[1]
    bf16, f32 = jnp.bfloat16, jnp.float32
    rows = HEADS * local
    dma = pltpu.SemaphoreType.DMA
    others = max(sibs - 1, 1)
    return pl.pallas_call(
        functools.partial(kernel, nz, tm),
        out_shape=pltpu.VMEM((local, width), bf16),
        in_specs=[pl.BlockSpec(memory_space=pl.ANY)] * 6
        + [pl.BlockSpec(memory_space=pltpu.SMEM)] * 2,
        out_specs=pl.BlockSpec(memory_space=pltpu.VMEM),
        scratch_shapes=[
            pltpu.VMEM((3, local, width), bf16),
            pltpu.VMEM((HEADS, 3 * local, HD), bf16),
            pltpu.VMEM((sibs, HEADS, 3 * local, HD), bf16),
            pltpu.VMEM((sibs, per_plane * SLOTS, 2 * HD), bf16),
            pltpu.VMEM((per_plane, SLOTS, 2 * HD), bf16),
            pltpu.VMEM((FRAMES, ROWS, LANES), bf16),
            pltpu.VMEM((FRAMES, LANES // HD, ROWS, HD), f32),
            pltpu.VMEM((COARSE, coarse_proj.shape[0]), f32),
            pltpu.VMEM((2 * fine_proj.shape[0], heads_width), bf16),
            pltpu.VMEM(coarse_proj.shape, bf16),
            pltpu.VMEM((rows, HD), bf16),
            pltpu.VMEM((HEADS, local, HD), bf16),
            pltpu.VMEM((rows, HD), f32),
            pltpu.VMEM((rows, HD), f32),
            pltpu.VMEM((rows, HD), f32),
            dma((HEADS,)),
            dma((HEADS,)),
            dma((3,)),
            dma((2, others)),
            dma((sibs, 2)),
            dma((per_plane,)),
            dma((per_plane,)),
            dma((others,)),
            dma((sibs,)),
            dma((HEADS,)),
            dma((HEADS,)),
            dma((KCHUNKS,)),
            dma((8, 2)),
            dma(()),
        ],
        compiler_params=pltpu.CompilerParams(
            collective_id=0, has_side_effects=True, vmem_limit_bytes=56 * 1024 * 1024
        ),
        cost_estimate=pl.CostEstimate(
            flops=700_000_000, bytes_accessed=12_000_000, transcendentals=1_100_000
        ),
    )(queries, keys, values, history, fine_proj, coarse_proj, frame_counts, levels)


def solution(mesh):
    in_specs = (
        P(("tm", "head"), None),
        P(("tm", "head"), None),
        P(("tm", "head"), None),
        P("tm", None, None, None),
        P(None, "head"),
        P(None, "head"),
        P(),
        P(),
    )
    out_specs = P(("tm", "head"), None)
    nz, tm = mesh.shape["head"], mesh.shape["tm"]
    return jax.shard_map(
        functools.partial(body, nz, tm),
        mesh=mesh,
        in_specs=in_specs,
        out_specs=out_specs,
        check_vma=False,
    )
```
